128 devices in a mesh: pipe: 2 (over x_hi), expert: 16 (over x_lo, y, core), tensor: 4 (over z).
Axes of the slice: x: 4 (x_hi: 2, x_lo: 2; x = x_hi * 2 + x_lo), y: 4, z: 4, core: 2. Of those that a mesh axis runs over, the one named last changes fastest.
Arguments:
- fwd_in: bfloat16 [2, 1024, 3072], P('pipe', 'expert', 'tensor'), may hold values from -6 to 6
- bwd_in: bfloat16 [2, 1024, 3072], P('pipe', 'expert', 'tensor'), may hold values from -6 to 6
- cotangent: bfloat16 [2, 1024, 3072], P('pipe', 'expert', 'tensor'), may hold values from -6 to 6
- route_fwd: int32 [2, 1024, 4], P('pipe', 'expert'), may hold values from 0 to 15, as said below
- gate_fwd: int32 [2, 1024, 4], P('pipe', 'expert'), may hold values from 4096 to 32767
- route_bwd: int32 [2, 1024, 4], P('pipe', 'expert'), may hold values from 0 to 15, as said below
- gate_bwd: int32 [2, 1024, 4], P('pipe', 'expert'), may hold values from 4096 to 32767
- w_gate: bfloat16 [2, 16, 5376, 3072], P('pipe', 'expert', 'tensor'), may hold values from -0.109375 to 0.109375
- w_up: bfloat16 [2, 16, 5376, 3072], P('pipe', 'expert', 'tensor'), may hold values from -0.109375 to 0.109375
- w_down: bfloat16 [2, 16, 5376, 3072], P('pipe', 'expert', 'tensor'), may hold values from -0.078125 to 0.078125
Outputs:
- next_inputs: bfloat16 [2, 1024, 3072], P('pipe', 'expert', 'tensor')
- next_grads: bfloat16 [2, 1024, 3072], P('pipe', 'expert', 'tensor')
The draws below stay inside these ranges and needn't reach their ends.
Inputs may be any that keep to these rules, and one draw needn't show every extreme that they name: `route_fwd`: each row names 4 different experts. Within each aligned block of 64 rows of a section no expert is named by more than 24 rows, and in each section one expert is named by exactly 24 rows of every block. `route_bwd`: each row names 4 different experts. Within each aligned block of 64 rows of a section no expert is named by more than 24 rows, and in each section one expert is named by exactly 24 rows of every block.
All inputs are finite; a program needn't handle non-finite values.
Results may differ from the reference program's by a relative error of at most 0.004.
Values may be sent and summed in bfloat16 or wider, within the bound.
No kernel may reach another device: no remote copies, remote signals or barrier semaphores. Data moves between devices by JAX's collectives and lax.ppermute only.
A program may use at most 128 MiB of HBM per device.

```python
import jax
import jax.numpy as jnp
from jax import lax

D = 3072
FF = 5376
TOP = 4
HALF_DEV = 64
EXPERTS = 16
CAP = 24
TOKENS = 1024


def route_block(key, hot_expert):
    key_order, key_shift, key_rows, key_turn = jax.random.split(key, 4)
    labels = jnp.arange(EXPERTS, dtype=jnp.int32)
    scores = jax.random.permutation(key_order, EXPERTS).astype(jnp.int32)
    scores = jnp.where(labels == hot_expert, EXPERTS, scores)
    ranking = jnp.argsort(scores).astype(jnp.int32)
    others = EXPERTS - 1
    spare = HALF_DEV * TOP - CAP
    base_count = spare // others
    extra_count = spare % others
    counts_other = base_count + (jnp.arange(others) < extra_count).astype(jnp.int32)
    pairs = others // 2
    move_top = max(0, min(base_count, CAP - base_count - 1)) + 1
    moved = jax.random.randint(key_shift, (pairs,), 0, move_top).astype(jnp.int32)
    shifts = jnp.zeros((others,), jnp.int32).at[0:2 * pairs:2].add(moved).at[1:2 * pairs:2].add(-moved)
    counts_other = counts_other + shifts
    counts = jnp.zeros((EXPERTS,), jnp.int32).at[ranking[:others]].set(counts_other).at[hot_expert].set(CAP)
    bounds = jnp.cumsum(counts)
    position = jnp.arange(HALF_DEV * TOP, dtype=jnp.int32)
    listed = jnp.sum((position[:, None] >= bounds[None, :]).astype(jnp.int32), axis=1)
    table = listed.reshape(TOP, HALF_DEV).T
    table = table[jax.random.permutation(key_rows, HALF_DEV)]
    turns = jax.random.randint(key_turn, (HALF_DEV, 1), 0, TOP).astype(jnp.int32)
    columns = (jnp.arange(TOP, dtype=jnp.int32)[None, :] + turns) % TOP
    return jnp.take_along_axis(table, columns, axis=1).astype(jnp.int32)


def section_routes(key):
    key_hot, key_blocks = jax.random.split(key)
    hot_expert = jax.random.randint(key_hot, (), 0, EXPERTS).astype(jnp.int32)
    block_keys = jax.random.split(key_blocks, TOKENS // HALF_DEV)
    return jax.vmap(route_block, in_axes=(0, None))(block_keys, hot_expert).reshape(TOKENS, TOP)


def draw_route_fwd(key, part):
    key = jax.random.fold_in(key, 11)
    return jnp.stack([section_routes(jax.random.fold_in(key, 0)), section_routes(jax.random.fold_in(key, 1))]).astype(jnp.int32)


def draw_route_bwd(key, part):
    key = jax.random.fold_in(key, 23)
    return jnp.stack([section_routes(jax.random.fold_in(key, 0)), section_routes(jax.random.fold_in(key, 1))]).astype(jnp.int32)


def touch_ends(result, key, smallest, largest):
    longest = result.shape.index(max(result.shape))
    spots = []
    for shift in (0, 1):
        where = [jax.random.randint(jax.random.fold_in(key, axis), (), 0, length) for axis, length in enumerate(result.shape)]
        where[longest] = (where[longest] + shift) % result.shape[longest]
        spots.append(tuple(where))
    return result.at[spots[0]].set(smallest).at[spots[1]].set(largest)


def levels(stream_key, shape, cuts, low, high):
    gain, own = 1.0, jax.random.fold_in(stream_key, 6)
    for dim, shards_of in cuts:
        steps = jnp.exp(jax.random.uniform(jax.random.fold_in(own, dim), (shards_of,), jnp.float32, low / len(cuts), high / len(cuts)))
        gain = gain * jnp.repeat(steps, shape[dim] // shards_of).reshape([-1 if axis == dim else 1 for axis in range(len(shape))])
    return gain


def normal_values(rng, extent, deviation, most, cuts=(), kind=jnp.bfloat16):
    level = levels(rng, extent, cuts, -0.22, 0.18) if cuts else 1.0
    drawn = jax.random.normal(rng, extent, jnp.float32) * deviation * level
    return jnp.minimum(jnp.maximum(drawn, -most), most).astype(kind)


def setup_inputs(seed: int = 0) -> dict:
    key_of = jax.random.split(jax.random.key(seed), 11)
    return {
        "fwd_in": normal_values(key_of[0], (2, TOKENS, D), 1.0, 6.0, ((0, 2), (1, 16), (2, 4))),
        "bwd_in": normal_values(key_of[1], (2, TOKENS, D), 1.0, 6.0, ((0, 2), (1, 16), (2, 4))),
        "cotangent": normal_values(key_of[2], (2, TOKENS, D), 1.0, 6.0, ((0, 2), (1, 16), (2, 4))),
        "route_fwd": draw_route_fwd(jax.random.fold_in(key_of[10], 71), 0),
        "gate_fwd": touch_ends(jax.random.randint(key_of[4], (2, TOKENS, TOP), 4096, 32768), jax.random.fold_in(key_of[4], 1), 4096, 32767).astype(jnp.int32),
        "route_bwd": draw_route_bwd(jax.random.fold_in(key_of[10], 71), 0),
        "gate_bwd": touch_ends(jax.random.randint(key_of[6], (2, TOKENS, TOP), 4096, 32768), jax.random.fold_in(key_of[6], 1), 4096, 32767).astype(jnp.int32),
        "w_gate": normal_values(key_of[7], (2, EXPERTS, FF, D), D ** -0.5, 0.109375, ((0, 2), (1, 16), (2, 4))),
        "w_up": normal_values(key_of[8], (2, EXPERTS, FF, D), D ** -0.5, 0.109375, ((0, 2), (1, 16), (2, 4))),
        "w_down": normal_values(key_of[9], (2, EXPERTS, FF, D), FF ** -0.5, 0.078125, ((0, 2), (1, 16), (2, 4))),
    }


def project_model(activations, weight):
    return jnp.dot(activations, weight.T, preferred_element_type=jnp.float32)


def expert_forward(activations, gate_weight, up_weight, down_weight):
    pre_gate = project_model(activations, gate_weight)
    pre_up = project_model(activations, up_weight)
    hidden = (jax.nn.silu(pre_gate) * pre_up).astype(jnp.bfloat16)
    return jnp.dot(hidden, down_weight, preferred_element_type=jnp.float32)


def expert_backward(activations, upstream, gate_weight, up_weight, down_weight):
    pre_gate = project_model(activations, gate_weight)
    pre_up = project_model(activations, up_weight)
    sigmoid_gate = jax.nn.sigmoid(pre_gate)
    hidden_grad = project_model(upstream, down_weight)
    gate_grad = (hidden_grad * pre_up * sigmoid_gate * (1.0 + pre_gate * (1.0 - sigmoid_gate))).astype(jnp.bfloat16)
    up_grad = (hidden_grad * pre_gate * sigmoid_gate).astype(jnp.bfloat16)
    return jnp.dot(gate_grad, gate_weight, preferred_element_type=jnp.float32) + jnp.dot(up_grad, up_weight, preferred_element_type=jnp.float32)


def slot_positions(route_rows):
    blocks = TOKENS // HALF_DEV
    flat_ids = route_rows.reshape(-1).astype(jnp.int32)
    one_hot = (flat_ids[:, None] == jnp.arange(EXPERTS, dtype=jnp.int32)[None, :]).astype(jnp.int32)
    grouped = one_hot.reshape(blocks, HALF_DEV * TOP, EXPERTS)
    earlier = (jnp.cumsum(grouped, axis=1) - grouped).astype(jnp.int32)
    slot_rank = jnp.sum(earlier * grouped, axis=2).reshape(-1).astype(jnp.int32)
    source = jnp.arange(TOKENS * TOP, dtype=jnp.int32) // (HALF_DEV * TOP)
    return (flat_ids * (blocks * CAP) + source * CAP + slot_rank).astype(jnp.int32)


def run_experts(kernel, operands, route_rows, weights):
    blocks = TOKENS // HALF_DEV
    slots = slot_positions(route_rows)
    capacity_all = EXPERTS * blocks * CAP
    token_index = jnp.arange(TOKENS * TOP, dtype=jnp.int32) // TOP
    table = jnp.zeros((capacity_all,), jnp.int32).at[slots].set(token_index)
    filled = jnp.zeros((capacity_all,), jnp.int32).at[slots].set(1)
    per_expert = tuple(
        jnp.where(filled[:, None] > 0, operand[table], jnp.zeros((), operand.dtype)).reshape(EXPERTS, blocks * CAP, -1)
        for operand in operands)
    results = lax.map(lambda bundle: kernel(*bundle), per_expert + weights)
    return results.astype(jnp.bfloat16).reshape(capacity_all, -1)[slots].reshape(TOKENS, TOP, -1)


def mix_terms(residual, gate_ints, picked):
    gate_values = gate_ints.astype(jnp.float32) / 65536.0
    mixed = jnp.sum(gate_values[:, :, None] * picked.astype(jnp.float32), axis=1)
    return (residual.astype(jnp.float32) + mixed).astype(jnp.bfloat16)


def reference(fwd_in, bwd_in, cotangent, route_fwd, gate_fwd, route_bwd, gate_bwd, w_gate, w_up, w_down):
    outputs = []
    gradients = []
    for section_index in range(2):
        weights = (w_gate[section_index], w_up[section_index], w_down[section_index])
        picked = run_experts(expert_forward, (fwd_in[section_index],), route_fwd[section_index], weights)
        outputs.append(mix_terms(fwd_in[section_index], gate_fwd[section_index], picked))
        picked_back = run_experts(expert_backward, (bwd_in[section_index], cotangent[section_index]), route_bwd[section_index], weights)
        gradients.append(mix_terms(cotangent[section_index], gate_bwd[section_index], picked_back))
    return jnp.roll(jnp.stack(outputs), 1, axis=0), jnp.roll(jnp.stack(gradients), -1, axis=0)
```

```python
import functools

import jax
import jax.numpy as jnp
from jax import lax
from jax.experimental import pallas as pl
from jax.experimental.pallas import tpu as pltpu
from jax.sharding import PartitionSpec as P

F32 = jnp.float32
BF16 = jnp.bfloat16
VMEM_LIMIT = 56 * 1024 * 1024


def params():
    return pltpu.CompilerParams(vmem_limit_bytes=VMEM_LIMIT)


def contract_last(rows, weight):
    return lax.dot_general(rows, weight, (((1,), (1,)), ((), ())), preferred_element_type=F32)


def contract_first(table, rows):
    return lax.dot_general(table, rows, (((0,), (0,)), ((), ())), preferred_element_type=F32)


def shift(shard, axis, by):
    length = lax.axis_size(axis)
    return lax.ppermute(shard, axis, [(i, (i + by) % length) for i in range(length)])


def after(value, *earlier):
    return lax.optimization_barrier((value, *earlier))[0]


def slot_tables(route, gate, experts, capacity):
    tokens, fanout = route.shape
    slots = experts * capacity
    labels = lax.broadcasted_iota(jnp.int32, (tokens, experts), 1)
    picks = [(route[:, k : k + 1] == labels).astype(F32) for k in range(fanout)]
    member = functools.reduce(jnp.add, picks)
    row = lax.broadcasted_iota(jnp.int32, (tokens, tokens), 0)
    column = lax.broadcasted_iota(jnp.int32, (tokens, tokens), 1)
    earlier = (column < row).astype(BF16)
    rank = jnp.dot(earlier, member.astype(BF16), preferred_element_type=F32)
    place = rank + (labels * capacity).astype(F32)
    slot_ids = lax.broadcasted_iota(jnp.int32, (tokens, slots), 1)
    table = jnp.zeros((tokens, slots), F32)
    high = jnp.zeros((tokens, slots), F32)
    low = jnp.zeros((tokens, slots), F32)
    for k in range(fanout):
        target = jnp.sum(picks[k] * place, axis=1, keepdims=True).astype(jnp.int32)
        hit = (slot_ids == target).astype(F32)
        gate_k = gate[:, k : k + 1]
        high_k = ((gate_k >> 7) << 7).astype(F32) * (1.0 / 65536.0)
        low_k = (gate_k & 127).astype(F32) * (1.0 / 65536.0)
        table += hit
        high += hit * high_k
        low += hit * low_k
    return table.astype(BF16), jnp.concatenate([high, low], axis=0).astype(BF16)


def dispatch_kernel(experts, capacity, rf, gf, rb, gb, f, c, send, table_b, mix_f, mix_b):
    quarter = f.shape[1]
    table, mix_f[...] = slot_tables(rf[...], gf[...], experts, capacity)
    send[:, :quarter] = contract_first(table, f[...]).astype(BF16)
    table, mix_b[...] = slot_tables(rb[...], gb[...], experts, capacity)
    table_b[...] = table
    send[:, quarter:] = contract_first(table, c[...]).astype(BF16)


def dispatch(rf, gf, rb, gb, f, c, experts, capacity):
    tokens, quarter = f.shape
    slots = experts * capacity
    return pl.pallas_call(
        functools.partial(dispatch_kernel, experts, capacity),
        out_shape=(
            jax.ShapeDtypeStruct((slots, 2 * quarter), BF16),
            jax.ShapeDtypeStruct((tokens, slots), BF16),
            jax.ShapeDtypeStruct((2 * tokens, slots), BF16),
            jax.ShapeDtypeStruct((2 * tokens, slots), BF16),
        ),
        compiler_params=params(),
    )(rf, gf, rb, gb, f, c)


def place_pieces(order, pieces, whole):
    quarter = pieces[0].shape[1]
    for n, piece in enumerate(pieces):
        whole[:, pl.ds(pl.multiple_of(order[n] * quarter, quarter), quarter)] = piece[...]


def dispatch_whole_kernel(order, table, p0, p1, p2, p3, send):
    quarter = p0.shape[1]
    for n, piece in enumerate((p0, p1, p2, p3)):
        rows = contract_first(table[...], piece[...]).astype(BF16)
        send[:, pl.ds(pl.multiple_of(order[n] * quarter, quarter), quarter)] = rows


def dispatch_whole(order, table, pieces):
    slots = table.shape[1]
    features = 4 * pieces[0].shape[1]
    vmem = pl.BlockSpec(memory_space=pltpu.VMEM)
    return pl.pallas_call(
        dispatch_whole_kernel,
        in_specs=[pl.BlockSpec(memory_space=pltpu.SMEM)] + [vmem] * 5,
        out_specs=vmem,
        out_shape=jax.ShapeDtypeStruct((slots, features), BF16),
        compiler_params=params(),
    )(order, table, *pieces)


def hidden_kernel(order, p0, p1, p2, p3, wg, wu, hidden, whole):
    @pl.when(pl.program_id(0) == 0)
    def _():
        place_pieces(order, (p0, p1, p2, p3), whole)

    rows = whole[...]
    a = contract_last(rows, wg[...])
    b = contract_last(rows, wu[...])
    hidden[0] = (a * jax.nn.sigmoid(a) * b).astype(BF16)


def hidden_forward(order, pieces, wg, wu, tile):
    rows, quarter = pieces[0].shape
    units, features = wg.shape
    weight = pl.BlockSpec((tile, features), lambda i: (i, 0))
    piece = pl.BlockSpec((rows, quarter), lambda i: (0, 0))
    return pl.pallas_call(
        hidden_kernel,
        grid=(units // tile,),
        in_specs=[pl.BlockSpec(memory_space=pltpu.SMEM)] + [piece] * 4 + [weight] * 2,
        out_specs=pl.BlockSpec((1, rows, tile), lambda i: (i, 0, 0)),
        out_shape=jax.ShapeDtypeStruct((units // tile, rows, tile), BF16),
        scratch_shapes=[pltpu.VMEM((rows, features), BF16)],
        compiler_params=params(),
        cost_estimate=pl.CostEstimate(
            flops=4 * rows * features * units, bytes_accessed=4 * units * features, transcendentals=rows * units
        ),
    )(order, *pieces, wg, wu)


def grads_kernel(order, x, p0, p1, p2, p3, wg, wu, wd, da, db, whole):
    @pl.when(pl.program_id(0) == 0)
    def _():
        place_pieces(order, (p0, p1, p2, p3), whole)

    rows = x[...]
    a = contract_last(rows, wg[...])
    b = contract_last(rows, wu[...])
    dh = contract_last(whole[...], wd[...])
    q = jax.nn.sigmoid(a)
    scaled = dh * q
    da[0] = (scaled * b * (1.0 + a * (1.0 - q))).astype(BF16)
    db[0] = (scaled * a).astype(BF16)


def hidden_grads(order, x, pieces, wg, wu, wd, tile):
    rows, quarter = pieces[0].shape
    units, features = wg.shape
    weight = pl.BlockSpec((tile, features), lambda i: (i, 0))
    piece = pl.BlockSpec((rows, quarter), lambda i: (0, 0))
    result = pl.BlockSpec((1, rows, tile), lambda i: (i, 0, 0))
    return pl.pallas_call(
        grads_kernel,
        grid=(units // tile,),
        in_specs=[pl.BlockSpec(memory_space=pltpu.SMEM), pl.BlockSpec((rows, features), lambda i: (0, 0))]
        + [piece] * 4
        + [weight] * 3,
        out_specs=[result, result],
        out_shape=[jax.ShapeDtypeStruct((units // tile, rows, tile), BF16)] * 2,
        scratch_shapes=[pltpu.VMEM((rows, features), BF16)],
        compiler_params=params(),
        cost_estimate=pl.CostEstimate(
            flops=6 * rows * features * units, bytes_accessed=6 * units * features, transcendentals=rows * units
        ),
    )(order, x, *pieces, wg, wu, wd)


def slices_kernel(pairs, order, *refs):
    acts, weights = refs[:pairs], refs[pairs : 2 * pairs]
    out, total = refs[2 * pairs], refs[2 * pairs + 1]
    step, last = pl.program_id(1), pl.num_programs(1) - 1
    part = functools.reduce(
        jnp.add, [jnp.dot(a[0], w[...], preferred_element_type=F32) for a, w in zip(acts, weights)]
    )

    @pl.when(step == 0)
    def _():
        total[...] = part

    @pl.when(step > 0)
    def _():
        total[...] += part

    @pl.when(step == last)
    def _():
        out[0] = total[...].astype(out.dtype)


def result_slices(order, acts, weights, quarter, dtype):
    tiles, rows, tile = acts[0].shape
    units = tiles * tile
    count = order.shape[0]
    act = pl.BlockSpec((1, rows, tile), lambda j, i, order: (i, 0, 0))
    weight = pl.BlockSpec((tile, quarter), lambda j, i, order: (i, order[j]))
    return pl.pallas_call(
        functools.partial(slices_kernel, len(acts)),
        grid_spec=pltpu.PrefetchScalarGridSpec(
            num_scalar_prefetch=1,
            grid=(count, tiles),
            in_specs=[act] * len(acts) + [weight] * len(acts),
            out_specs=pl.BlockSpec((1, rows, quarter), lambda j, i, order: (j, 0, 0)),
            scratch_shapes=[pltpu.VMEM((rows, quarter), F32)],
        ),
        out_shape=jax.ShapeDtypeStruct((count, rows, quarter), dtype),
        compiler_params=params(),
        cost_estimate=pl.CostEstimate(
            flops=2 * count * len(acts) * rows * quarter * units,
            bytes_accessed=2 * count * len(acts) * units * quarter,
            transcendentals=0,
        ),
    )(order, *acts, *weights)


def summed_over_tensor(place, acts, weights, quarter):
    order = (place + jnp.array([2, 1, 3, 0], jnp.int32)) % 4
    rows = acts[0].shape[1]
    half = rows // 2
    opposite = result_slices(order[:1], acts, weights, quarter, BF16)[0]
    up = shift(opposite[:half], "tensor", 1)
    down = shift(opposite[half:], "tensor", -1)
    sides = result_slices(order[1:3], acts, weights, quarter, BF16)
    own = result_slices(order[3:], acts, weights, quarter, F32)[0]
    to_next = jnp.concatenate([(sides[0, :half].astype(F32) + up.astype(F32)).astype(BF16), sides[0, half:]])
    to_last = jnp.concatenate([sides[1, :half], (sides[1, half:].astype(F32) + down.astype(F32)).astype(BF16)])
    from_last = shift(to_next, "tensor", 1)
    from_next = shift(to_last, "tensor", -1)
    return (own + from_last.astype(F32) + from_next.astype(F32)).astype(BF16)


def mix_kernel(mix, back, residual, out):
    tokens = residual.shape[0]
    both = jnp.dot(mix[...], back[...], preferred_element_type=F32)
    out[...] = (residual[...].astype(F32) + (both[:tokens] + both[tokens:])).astype(BF16)


def mixed(mix, back, residual):
    return pl.pallas_call(
        mix_kernel, out_shape=jax.ShapeDtypeStruct(residual.shape, BF16), compiler_params=params()
    )(mix, back, residual)


def exchange(rows):
    return lax.all_to_all(rows, "expert", split_axis=0, concat_axis=0, tiled=True)


def local(fwd_in, bwd_in, cotangent, route_fwd, gate_fwd, route_bwd, gate_bwd, w_gate, w_up, w_down):
    experts = lax.axis_size("expert")
    f, x, c = fwd_in[0], bwd_in[0], cotangent[0]
    tokens, quarter = f.shape
    fanout = route_fwd.shape[2]
    capacity = min(tokens, max(2, tokens * fanout * 3 // (2 * experts)))
    wg, wu, wd = w_gate[0, 0], w_up[0, 0], w_down[0, 0]
    tile = wg.shape[0] // 3
    place = lax.axis_index("tensor").astype(jnp.int32)
    order = (place + jnp.array([0, 3, 1, 2], jnp.int32)) % 4

    send_fc, table_b, mix_f, mix_b = dispatch(
        route_fwd[0], gate_fwd[0], route_bwd[0], gate_bwd[0], f, c, experts, capacity
    )
    x_pieces = (x, shift(x, "tensor", 1), shift(x, "tensor", -1), shift(x, "tensor", 2))
    got_fc = exchange(send_fc)
    send_x = dispatch_whole(order, table_b, x_pieces)
    rows_x = exchange(after(send_x, got_fc))

    f0, c0 = got_fc[:, :quarter], got_fc[:, quarter:]
    f_last, f_next = shift(f0, "tensor", 1), shift(f0, "tensor", -1)
    f_opposite = shift(f_last, "tensor", 1)
    c1 = after(c0, f_next)
    c_next = shift(c1, "tensor", -1)
    c_opposite = shift(c_next, "tensor", -1)
    c_last = shift(after(c0, f_opposite), "tensor", 1)

    hidden = hidden_forward(order, (f0, f_last, f_next, f_opposite), wg, wu, tile)
    share_f = summed_over_tensor(place, (hidden,), (wd,), quarter)
    da, db = hidden_grads(order, rows_x, (c0, c_last, c_next, c_opposite), wg, wu, wd, tile)
    share_b = summed_over_tensor(place, (da, db), (wg, wu), quarter)
    out_f = mixed(mix_f, exchange(share_f), f)
    out_b = mixed(mix_b, exchange(share_b), c)
    return shift(out_f[None], "pipe", 1), shift(out_b[None], "pipe", -1)


def solution(mesh):
    rows = P("pipe", "expert", "tensor")
    routes = P("pipe", "expert", None)
    weights = P("pipe", "expert", "tensor", None)
    return jax.shard_map(
        local,
        mesh=mesh,
        in_specs=(rows, rows, rows, routes, routes, routes, routes, weights, weights, weights),
        out_specs=(rows, rows),
        check_vma=False,
    )
```

```python
import functools

import jax
import jax.numpy as jnp
from jax import lax
from jax.experimental import pallas as pl
from jax.experimental.pallas import tpu as pltpu
from jax.sharding import PartitionSpec as P

F32 = jnp.float32
BF16 = jnp.bfloat16
VMEM = pl.BlockSpec(memory_space=pltpu.VMEM)
SMEM = pl.BlockSpec(memory_space=pltpu.SMEM)
ANY = pl.BlockSpec(memory_space=pl.ANY)


def params(mebibytes=12):
    return pltpu.CompilerParams(vmem_limit_bytes=mebibytes * 1024 * 1024)


def near(array):
    return pltpu.with_memory_space_constraint(array, pltpu.VMEM)


def far(array):
    return pltpu.with_memory_space_constraint(array, pltpu.HBM)


def contract_last(rows, weight):
    return lax.dot_general(rows, weight, (((1,), (1,)), ((), ())), preferred_element_type=F32)


def shift(shard, axis, by):
    length = lax.axis_size(axis)
    return lax.ppermute(shard, axis, [(i, (i + by) % length) for i in range(length)])


def after(value, *earlier):
    return lax.optimization_barrier((value, *earlier))[0]


def slot_tables(route, gate, experts, capacity):
    fanout, tokens = route.shape
    slots = experts * capacity
    labels = lax.broadcasted_iota(jnp.int32, (experts, tokens), 0)
    picks = [(route[k : k + 1, :] == labels).astype(F32) for k in range(fanout)]
    member = functools.reduce(jnp.add, picks)
    row = lax.broadcasted_iota(jnp.int32, (tokens, tokens), 0)
    column = lax.broadcasted_iota(jnp.int32, (tokens, tokens), 1)
    earlier = (row < column).astype(BF16)
    rank = jnp.dot(member.astype(BF16), earlier, preferred_element_type=F32)
    place = rank + (labels * capacity).astype(F32)
    slot_ids = lax.broadcasted_iota(jnp.int32, (slots, tokens), 0)
    table = jnp.zeros((slots, tokens), F32)
    high = jnp.zeros((slots, tokens), F32)
    low = jnp.zeros((slots, tokens), F32)
    for k in range(fanout):
        target = jnp.sum(picks[k] * place, axis=0, keepdims=True).astype(jnp.int32)
        hit = (slot_ids == target).astype(F32)
        gate_k = gate[k : k + 1, :]
        high_k = ((gate_k >> 7) << 7).astype(F32) * (1.0 / 65536.0)
        low_k = (gate_k & 127).astype(F32) * (1.0 / 65536.0)
        table += hit
        high += hit * high_k
        low += hit * low_k
    return table.astype(BF16), jnp.concatenate([high, low], axis=1).astype(BF16)


def dispatch_kernel(experts, capacity, rf, gf, rb, gb, f, x, send, table_b, mix_f, mix_b):
    quarter = f.shape[1]
    table, mix_f[...] = slot_tables(rf[...], gf[...], experts, capacity)
    send[:, :quarter] = jnp.dot(table, f[...], preferred_element_type=F32).astype(BF16)
    table, mix_b[...] = slot_tables(rb[...], gb[...], experts, capacity)
    table_b[...] = table
    send[:, quarter:] = jnp.dot(table, x[...], preferred_element_type=F32).astype(BF16)


def dispatch(rf, gf, rb, gb, f, x, experts, capacity):
    tokens, quarter = f.shape
    slots = experts * capacity
    return pl.pallas_call(
        functools.partial(dispatch_kernel, experts, capacity),
        out_shape=(
            pltpu.HBM((slots, 2 * quarter), BF16),
            pltpu.HBM((slots, tokens), BF16),
            pltpu.HBM((slots, 2 * tokens), BF16),
            pltpu.HBM((slots, 2 * tokens), BF16),
        ),
        compiler_params=params(),
    )(*[far(array) for array in (rf, gf, rb, gb, f, x)])


def dispatch_whole_kernel(order, table, p0, p1, p2, p3, send):
    quarter = p0.shape[1]
    for n, piece in enumerate((p0, p1, p2, p3)):
        rows = jnp.dot(table[...], piece[...], preferred_element_type=F32).astype(BF16)
        send[:, pl.ds(pl.multiple_of(order[n] * quarter, quarter), quarter)] = rows


def dispatch_whole(order, table, pieces):
    slots = table.shape[0]
    features = 4 * pieces[0].shape[1]
    return pl.pallas_call(
        dispatch_whole_kernel,
        in_specs=[SMEM] + [VMEM] * 5,
        out_specs=VMEM,
        out_shape=pltpu.HBM((slots, features), BF16),
        compiler_params=params(),
    )(order, table, *pieces)


def tiles(units, tile=256):
    return [(start, min(tile, units - start)) for start in range(0, units, tile)]


def columns(number, quarter):
    return pl.ds(pl.multiple_of(number * quarter, quarter), quarter)


def load_kernel(*refs):
    count = (len(refs) - 2) // 2
    mark, semaphores = refs[-2:]
    copies = [pltpu.make_async_copy(refs[n], refs[count + n], semaphores.at[n]) for n in range(count)]
    for copy in copies:
        copy.start()
    mark[...] = jnp.zeros_like(mark)
    for copy in copies:
        copy.wait()


def load_weights(weights):
    return pl.pallas_call(
        load_kernel,
        in_specs=[ANY] * len(weights),
        out_specs=[VMEM] * (len(weights) + 1),
        out_shape=[pltpu.VMEM(weight.shape, weight.dtype) for weight in weights]
        + [jax.ShapeDtypeStruct((8, 128), F32)],
        scratch_shapes=[pltpu.SemaphoreType.DMA((len(weights),))],
        compiler_params=params(2),
        cost_estimate=pl.CostEstimate(
            flops=0, bytes_accessed=sum(weight.size * 2 for weight in weights), transcendentals=0
        ),
    )(*[far(weight) for weight in weights])


def held_kernel(*refs):
    pass


def held(array, *earlier):
    return pl.pallas_call(
        held_kernel,
        in_specs=[ANY] * (1 + len(earlier)),
        out_specs=ANY,
        out_shape=jax.ShapeDtypeStruct(array.shape, array.dtype),
        input_output_aliases={0: 0},
        compiler_params=params(2),
        cost_estimate=pl.CostEstimate(flops=0, bytes_accessed=16 * 1024 * 1024, transcendentals=0),
    )(array, *earlier)


def halves_kernel(from_last, from_next, *refs):
    top, bottom = refs[-2:]
    half = top.shape[0]
    top[...] = from_last[:half]
    bottom[...] = from_next[half:]


def halves(from_last, from_next, *earlier):
    rows, quarter = from_last.shape
    return pl.pallas_call(
        halves_kernel,
        in_specs=[VMEM] * 2 + [ANY] * len(earlier),
        out_specs=[VMEM] * 2,
        out_shape=[jax.ShapeDtypeStruct((rows // 2, quarter), from_last.dtype)] * 2,
        compiler_params=params(4),
    )(from_last, from_next, *earlier)


def piece_sums(order, first_entry, pieces, wg, wu, part):
    quarter = pieces[0].shape[1]
    sums = []
    for weight in (wg, wu):
        terms = [
            contract_last(piece[...], weight[part, columns(order[first_entry + n], quarter)])
            for n, piece in enumerate(pieces)
        ]
        sums.append(functools.reduce(jnp.add, terms))
    return sums


def begin_kernel(order, p0, p1, p2, wg, wu, sum_a, sum_b):
    for start, size in tiles(wg.shape[0]):
        part = slice(start, start + size)
        sum_a[:, part], sum_b[:, part] = piece_sums(order, 0, (p0, p1, p2), wg, wu, part)


def begin_loading_kernel(order, p0, p1, p2, wg, wu, wd, sum_a, sum_b, near_g, near_u, near_d, semaphores):
    spans = load_spans(wg.shape[0])
    copies = []
    for p, (start, size) in enumerate(spans):
        span = pl.ds(start, size)
        copies.append(
            [
                pltpu.make_async_copy(wg.at[span, :], near_g.at[span, :], semaphores.at[p, 0]),
                pltpu.make_async_copy(wu.at[span, :], near_u.at[span, :], semaphores.at[p, 1]),
            ]
        )
    copies.append([pltpu.make_async_copy(wd, near_d, semaphores.at[len(spans), 0])])
    for copy in copies[0] + copies[1]:
        copy.start()
    for p, (begin, length) in enumerate(spans):
        for copy in copies[p]:
            copy.wait()
        if p + 2 < len(copies):
            for copy in copies[p + 2]:
                copy.start()
        for start, size in tiles(length):
            part = slice(begin + start, begin + start + size)
            sum_a[:, part], sum_b[:, part] = piece_sums(order, 0, (p0, p1, p2), near_g, near_u, part)
    copies[-1][0].wait()


def begin(order, pieces, weights):
    loading = len(weights) == 3
    rows, quarter = pieces[0].shape
    units = weights[0].shape[0]
    return pl.pallas_call(
        begin_loading_kernel if loading else begin_kernel,
        in_specs=[SMEM] + [VMEM] * 3 + [ANY if loading else VMEM] * len(weights),
        out_specs=[VMEM] * (5 if loading else 2),
        out_shape=[pltpu.VMEM((rows, units), F32)] * 2
        + ([pltpu.VMEM(w.shape, w.dtype) for w in weights] if loading else []),
        scratch_shapes=[pltpu.SemaphoreType.DMA((len(load_spans(units)) + 1, 2))] if loading else [],
        compiler_params=params(),
        cost_estimate=pl.CostEstimate(
            flops=12 * rows * quarter * units, bytes_accessed=12 * units * quarter, transcendentals=0
        ),
    )(order, *pieces, *[(far if loading else near)(w) for w in weights])


def finish_kernel(forward, order, top, bottom, sum_a, sum_b, wg, wu, *outs):
    rows = outs[-1]
    half = top.shape[0]
    rows[:half] = top[...]
    rows[half:] = bottom[...]
    for start, size in tiles(wg.shape[0]):
        part = slice(start, start + size)
        a, b = piece_sums(order, 3, (rows,), wg, wu, part)
        a += sum_a[:, part]
        b += sum_b[:, part]
        q = jax.nn.sigmoid(a)
        if forward:
            outs[0][:, part] = (a * q * b).astype(BF16)
        else:
            outs[0][:, part] = b * q * (1.0 + a * (1.0 - q))
            outs[1][:, part] = a * q


def finish(forward, order, halves, sums, wg, wu):
    rows, units = sums[0].shape
    quarter = halves[0].shape[1]
    outs = [pltpu.VMEM((rows, units), BF16)] if forward else [pltpu.VMEM((rows, units), F32)] * 2
    return pl.pallas_call(
        functools.partial(finish_kernel, forward),
        in_specs=[SMEM] + [VMEM] * 6,
        out_specs=[VMEM] * len(outs),
        out_shape=outs,
        scratch_shapes=[pltpu.VMEM((rows, quarter), BF16)],
        compiler_params=params(),
        cost_estimate=pl.CostEstimate(
            flops=4 * rows * quarter * units, bytes_accessed=4 * units * quarter, transcendentals=rows * units
        ),
    )(order, *halves, *[near(array) for array in (*sums, wg, wu)])


def load_spans(units):
    cuts = [0, min(256, units), min(768, units), units]
    return [(low, high - low) for low, high in zip(cuts, cuts[1:]) if high > low]


def grads_kernel(c, for_gate, for_up, wd, da, db):
    for start, size in tiles(wd.shape[0]):
        part = slice(start, start + size)
        dh = contract_last(c[...], wd[part, :])
        da[:, part] = (dh * for_gate[:, part]).astype(BF16)
        db[:, part] = (dh * for_up[:, part]).astype(BF16)


def hidden_grads(c, for_gate, for_up, wd):
    rows, features = c.shape
    units = wd.shape[0]
    return pl.pallas_call(
        grads_kernel,
        in_specs=[VMEM] * 4,
        out_specs=[VMEM] * 2,
        out_shape=[pltpu.VMEM((rows, units), BF16)] * 2,
        compiler_params=params(),
        cost_estimate=pl.CostEstimate(
            flops=2 * rows * features * units, bytes_accessed=2 * units * features, transcendentals=0
        ),
    )(c, near(for_gate), near(for_up), near(wd))


def down_kernel(which, pairs, order, *refs):
    acts, weights, outs = refs[:pairs], refs[pairs : 2 * pairs], refs[2 * pairs :]
    quarter = weights[0].shape[1] // 4
    for n, entry in enumerate(which):
        slots = columns(order[entry], quarter)
        total = functools.reduce(
            jnp.add, [jnp.dot(a[...], w[:, slots], preferred_element_type=F32) for a, w in zip(acts, weights)]
        )
        if len(which) == 4:
            outs[0][:, slots] = total.astype(outs[0].dtype)
        elif len(which) == 1:
            half = outs[0].shape[0]
            outs[0][...] = total[:half].astype(outs[0].dtype)
            outs[1][...] = total[half:].astype(outs[1].dtype)
        else:
            outs[n][...] = total.astype(outs[n].dtype)


def down_projections(order, which, acts, weights, outs):
    rows, units = acts[0].shape
    quarter = weights[0].shape[1] // 4
    pairs = len(acts)
    return pl.pallas_call(
        functools.partial(down_kernel, which, pairs),
        in_specs=[SMEM] + [VMEM] * (2 * pairs),
        out_specs=[VMEM] * len(outs),
        out_shape=outs,
        compiler_params=params(),
        cost_estimate=pl.CostEstimate(
            flops=2 * len(which) * pairs * rows * units * quarter,
            bytes_accessed=2 * len(which) * pairs * units * quarter,
            transcendentals=0,
        ),
    )(order, *[near(array) for array in (*acts, *weights)])


def passed_kernel(to_next, to_last, up, down, next_sum, last_sum):
    half = up.shape[0]
    next_sum[:half] = (to_next[:half].astype(F32) + up[...].astype(F32)).astype(BF16)
    next_sum[half:] = to_next[half:]
    last_sum[:half] = to_last[:half]
    last_sum[half:] = (to_last[half:].astype(F32) + down[...].astype(F32)).astype(BF16)


def total_kernel(own, from_last, from_next, out):
    out[...] = (own[...] + from_last[...].astype(F32) + from_next[...].astype(F32)).astype(BF16)


def summed_over_tensor(order, acts, weights, earlier):
    rows = acts[0].shape[0]
    quarter = weights[0].shape[1] // 4
    whole = jax.ShapeDtypeStruct((rows, quarter), BF16)
    half = jax.ShapeDtypeStruct((rows // 2, quarter), BF16)
    top, bottom = down_projections(order, (3,), acts, weights, [half, half])
    up = shift(top, "tensor", 1)
    down = shift(bottom, "tensor", -1)
    kept = [pltpu.VMEM(whole.shape, BF16)] * 2 + [pltpu.VMEM(whole.shape, F32)]
    to_next, to_last, own = down_projections(order, (2, 1, 0), acts, weights, kept)
    to_next, to_last = pl.pallas_call(passed_kernel, out_shape=[whole, whole], compiler_params=params())(
        near(to_next), near(to_last), up, down
    )
    from_last = shift(to_next, "tensor", 1)
    from_next = shift(to_last, "tensor", -1)
    from_next = after(from_next, *earlier)
    return pl.pallas_call(total_kernel, out_shape=whole, compiler_params=params())(near(own), from_last, from_next)


def mix(table, back):
    both = lax.dot_general(table, back, (((0,), (0,)), ((), ())), preferred_element_type=F32)
    tokens = both.shape[0] // 2
    return both[:tokens] + both[tokens:]


def mix_kernel(table, back, residual, out):
    out[...] = (residual[...].astype(F32) + mix(table[...], back[...])).astype(BF16)


def mixed(table, back, residual):
    return pl.pallas_call(
        mix_kernel, out_shape=jax.ShapeDtypeStruct(residual.shape, BF16), compiler_params=params()
    )(table, back, residual)


def mix_parts_kernel(order, table, back, residual, own, to_last, to_next, to_opposite):
    quarter = residual.shape[1]
    own[...] = residual[...].astype(F32) + mix(table[...], back[:, columns(order[0], quarter)])
    for entry, out in ((1, to_last), (2, to_next), (3, to_opposite)):
        out[...] = mix(table[...], back[:, columns(order[entry], quarter)]).astype(BF16)


def mixed_over_tensor(order, table, back, residual):
    part = jax.ShapeDtypeStruct(residual.shape, BF16)
    own, to_last, to_next, to_opposite = pl.pallas_call(
        mix_parts_kernel,
        in_specs=[SMEM] + [VMEM] * 3,
        out_specs=[VMEM] * 4,
        out_shape=[jax.ShapeDtypeStruct(residual.shape, F32), part, part, part],
        compiler_params=params(),
    )(order, table, back, residual)
    return own, to_last, to_next, to_opposite


def total_over_tensor(own, to_last, to_next, to_opposite):
    received = (shift(to_last, "tensor", -1), shift(to_next, "tensor", 1), shift(to_opposite, "tensor", 2))
    return (own + sum(piece.astype(F32) for piece in received)).astype(BF16)


def exchange(rows):
    return lax.all_to_all(rows, "expert", split_axis=0, concat_axis=0, tiled=True)


def local(fwd_in, bwd_in, cotangent, route_fwd, gate_fwd, route_bwd, gate_bwd, w_gate, w_up, w_down):
    experts = lax.axis_size("expert")
    f, x, c = fwd_in[0], bwd_in[0], cotangent[0]
    tokens, quarter = f.shape
    fanout = route_fwd.shape[2]
    capacity = min(tokens, max(2, tokens * fanout * 3 // (2 * experts)))
    place = lax.axis_index("tensor").astype(jnp.int32)
    order = (place + jnp.array([0, 3, 1, 2], jnp.int32)) % 4

    c_pieces = (c, shift(c, "tensor", 1), shift(c, "tensor", -1), shift(c, "tensor", 2))
    send, table_b, mix_f, mix_b = dispatch(
        route_fwd[0].T, gate_fwd[0].T, route_bwd[0].T, gate_bwd[0].T, f, x, experts, capacity
    )
    wg, wu, wd = w_gate[0, 0], w_up[0, 0], w_down[0, 0]
    got = exchange(send)
    send_c = dispatch_whole(order, table_b, c_pieces)
    got, send_c = lax.optimization_barrier((got, send_c))
    f0, x0 = got[:, :quarter], got[:, quarter:]
    rows_c = exchange(after(send_c, f0, x0))
    f_last, f_next = shift(f0, "tensor", 1), shift(f0, "tensor", -1)
    near_g, near_u, near_d, loaded = load_weights((wg, wu, wd))
    f_top, f_bottom = halves(f_last, f_next, loaded)
    f_opposite = shift(f_top, "tensor", 1), shift(f_bottom, "tensor", -1)
    x0 = held(x0, f_top, f_bottom)
    x_next, x_last = shift(x0, "tensor", -1), shift(x0, "tensor", 1)
    x_top, x_bottom = halves(x_last, x_next)
    x_opposite = shift(x_top, "tensor", 1), shift(x_bottom, "tensor", -1)

    sums = begin(order, (f0, f_last, f_next), (near_g, near_u))
    (hidden,) = finish(True, order, f_opposite, sums, near_g, near_u)
    whole = pltpu.HBM((hidden.shape[0], wd.shape[1]), BF16)
    (part_f,) = down_projections(order, (0, 1, 2, 3), (hidden,), (near_d,), [whole])
    back_f = exchange(part_f)
    *sums, near_g, near_u, near_d = begin(order, (held(x0, part_f), x_last, x_next), (wg, wu, wd))
    for_gate, for_up = finish(False, order, x_opposite, sums, near_g, near_u)
    da, db = hidden_grads(rows_c, for_gate, for_up, near_d)
    mixed_f = mixed_over_tensor(order, mix_f, back_f, f)
    share_b = summed_over_tensor(order, (da, db), (near_g, near_u), mixed_f)
    out_f = total_over_tensor(*mixed_f)
    out_b = mixed(mix_b, exchange(share_b), c)
    return shift(out_f[None], "pipe", 1), shift(out_b[None], "pipe", -1)


def solution(mesh):
    rows = P("pipe", "expert", "tensor")
    routes = P("pipe", "expert", None)
    weights = P("pipe", "expert", "tensor", None)
    return jax.shard_map(
        local,
        mesh=mesh,
        in_specs=(rows, rows, rows, routes, routes, routes, routes, weights, weights, weights),
        out_specs=(rows, rows),
        check_vma=False,
    )
```

```python
import functools

import jax
import jax.numpy as jnp
from jax import lax
from jax.experimental import pallas as pl
from jax.experimental.pallas import tpu as pltpu
from jax.sharding import PartitionSpec as P

F32 = jnp.float32
BF16 = jnp.bfloat16
VMEM = pl.BlockSpec(memory_space=pltpu.VMEM)
SMEM = pl.BlockSpec(memory_space=pltpu.SMEM)
ANY = pl.BlockSpec(memory_space=pl.ANY)


def params(mebibytes=8):
    return pltpu.CompilerParams(vmem_limit_bytes=mebibytes * 1024 * 1024)


def near(array):
    return pltpu.with_memory_space_constraint(array, pltpu.VMEM)


def far(array):
    return pltpu.with_memory_space_constraint(array, pltpu.HBM)


def contract_last(rows, weight):
    return lax.dot_general(rows, weight, (((1,), (1,)), ((), ())), preferred_element_type=F32)


def shift(shard, axis, by):
    length = lax.axis_size(axis)
    return lax.ppermute(shard, axis, [(i, (i + by) % length) for i in range(length)])


def after(value, *earlier):
    return lax.optimization_barrier((value, *earlier))[0]


def slot_tables(route, gate, experts, capacity):
    fanout, tokens = route.shape
    slots = experts * capacity
    labels = lax.broadcasted_iota(jnp.int32, (experts, tokens), 0)
    picks = [(route[k : k + 1, :] == labels).astype(F32) for k in range(fanout)]
    member = functools.reduce(jnp.add, picks)
    row = lax.broadcasted_iota(jnp.int32, (tokens, tokens), 0)
    column = lax.broadcasted_iota(jnp.int32, (tokens, tokens), 1)
    earlier = (row < column).astype(BF16)
    rank = jnp.dot(member.astype(BF16), earlier, preferred_element_type=F32)
    place = rank + (labels * capacity).astype(F32)
    slot_ids = lax.broadcasted_iota(jnp.int32, (slots, tokens), 0)
    table = jnp.zeros((slots, tokens), F32)
    high = jnp.zeros((slots, tokens), F32)
    low = jnp.zeros((slots, tokens), F32)
    for k in range(fanout):
        target = jnp.sum(picks[k] * place, axis=0, keepdims=True).astype(jnp.int32)
        hit = (slot_ids == target).astype(F32)
        gate_k = gate[k : k + 1, :]
        high_k = ((gate_k >> 7) << 7).astype(F32) * (1.0 / 65536.0)
        low_k = (gate_k & 127).astype(F32) * (1.0 / 65536.0)
        table += hit
        high += hit * high_k
        low += hit * low_k
    return table.astype(BF16), jnp.concatenate([high, low], axis=1).astype(BF16)


def dispatch_kernel(experts, capacity, rf, gf, rb, gb, f, x, send, table_b, mix_f, mix_b):
    quarter = f.shape[1]
    table, mix_f[...] = slot_tables(rf[...], gf[...], experts, capacity)
    send[:, :quarter] = jnp.dot(table, f[...], preferred_element_type=F32).astype(BF16)
    table, mix_b[...] = slot_tables(rb[...], gb[...], experts, capacity)
    table_b[...] = table
    send[:, quarter:] = jnp.dot(table, x[...], preferred_element_type=F32).astype(BF16)


def dispatch(rf, gf, rb, gb, f, x, experts, capacity):
    tokens, quarter = f.shape
    slots = experts * capacity
    return pl.pallas_call(
        functools.partial(dispatch_kernel, experts, capacity),
        out_shape=(
            pltpu.HBM((slots, 2 * quarter), BF16),
            pltpu.HBM((slots, tokens), BF16),
            pltpu.HBM((slots, 2 * tokens), BF16),
            pltpu.HBM((slots, 2 * tokens), BF16),
        ),
        compiler_params=params(),
    )(*[far(array) for array in (rf, gf, rb, gb, f, x)])


def dispatch_whole_kernel(order, table, p0, p1, p2, p3, send):
    quarter = p0.shape[1]
    for n, piece in enumerate((p0, p1, p2, p3)):
        rows = jnp.dot(table[...], piece[...], preferred_element_type=F32).astype(BF16)
        send[:, pl.ds(pl.multiple_of(order[n] * quarter, quarter), quarter)] = rows


def dispatch_whole(order, table, pieces):
    slots = table.shape[0]
    features = 4 * pieces[0].shape[1]
    return pl.pallas_call(
        dispatch_whole_kernel,
        in_specs=[SMEM] + [VMEM] * 5,
        out_specs=VMEM,
        out_shape=pltpu.HBM((slots, features), BF16),
        compiler_params=params(),
    )(order, table, *pieces)


def tiles(units, tile=256):
    return [(start, min(tile, units - start)) for start in range(0, units, tile)]


def columns(number, quarter):
    return pl.ds(pl.multiple_of(number * quarter, quarter), quarter)


def load_kernel(*refs):
    count = (len(refs) - 2) // 2
    mark, semaphores = refs[-2:]
    copies = [pltpu.make_async_copy(refs[n], refs[count + n], semaphores.at[n]) for n in range(count)]
    for copy in copies:
        copy.start()
    mark[...] = jnp.zeros_like(mark)
    for copy in copies:
        copy.wait()


def load_weights(weights):
    return pl.pallas_call(
        load_kernel,
        in_specs=[ANY] * len(weights),
        out_specs=[VMEM] * (len(weights) + 1),
        out_shape=[pltpu.VMEM(weight.shape, weight.dtype) for weight in weights]
        + [jax.ShapeDtypeStruct((8, 128), F32)],
        scratch_shapes=[pltpu.SemaphoreType.DMA((len(weights),))],
        compiler_params=params(2),
        cost_estimate=pl.CostEstimate(
            flops=0, bytes_accessed=sum(weight.size * 2 for weight in weights), transcendentals=0
        ),
    )(*[far(weight) for weight in weights])


def held_kernel(*refs):
    pass


def held(array, *earlier):
    return pl.pallas_call(
        held_kernel,
        in_specs=[ANY] * (1 + len(earlier)),
        out_specs=ANY,
        out_shape=jax.ShapeDtypeStruct(array.shape, array.dtype),
        input_output_aliases={0: 0},
        compiler_params=params(2),
        cost_estimate=pl.CostEstimate(flops=0, bytes_accessed=16 * 1024 * 1024, transcendentals=0),
    )(array, *earlier)


def halves_kernel(from_last, from_next, *refs):
    top, bottom = refs[-2:]
    half = top.shape[0]
    top[...] = from_last[:half]
    bottom[...] = from_next[half:]


def halves(from_last, from_next, *earlier):
    rows, quarter = from_last.shape
    return pl.pallas_call(
        halves_kernel,
        in_specs=[VMEM] * 2 + [ANY] * len(earlier),
        out_specs=[VMEM] * 2,
        out_shape=[jax.ShapeDtypeStruct((rows // 2, quarter), from_last.dtype)] * 2,
        compiler_params=params(4),
    )(from_last, from_next, *earlier)


def piece_sums(order, first_entry, pieces, wg, wu, part):
    quarter = pieces[0].shape[1]
    sums = []
    for weight in (wg, wu):
        terms = [
            contract_last(piece[...], weight[part, columns(order[first_entry + n], quarter)])
            for n, piece in enumerate(pieces)
        ]
        sums.append(functools.reduce(jnp.add, terms))
    return sums


def begin_kernel(first_entry, count, order, *refs):
    pieces, (wg, wu), earlier, (sum_a, sum_b, mark) = refs[:count], refs[count : count + 2], refs[count + 2 : -3], refs[-3:]
    mark[...] = jnp.zeros_like(mark)
    for start, size in tiles(wg.shape[0]):
        part = slice(start, start + size)
        a, b = piece_sums(order, first_entry, pieces, wg, wu, part)
        if earlier:
            a += earlier[0][:, part]
            b += earlier[1][:, part]
        sum_a[:, part] = a
        sum_b[:, part] = b


def begin(order, first_entry, pieces, wg, wu, earlier):
    rows, quarter = pieces[0].shape
    units = wg.shape[0]
    count = len(pieces)
    return pl.pallas_call(
        functools.partial(begin_kernel, first_entry, count),
        in_specs=[SMEM] + [VMEM] * (count + 2 + len(earlier)),
        out_specs=[VMEM] * 3,
        out_shape=[pltpu.VMEM((rows, units), F32)] * 2 + [jax.ShapeDtypeStruct((8, 128), F32)],
        compiler_params=params(),
        cost_estimate=pl.CostEstimate(
            flops=4 * count * rows * quarter * units, bytes_accessed=4 * count * units * quarter, transcendentals=0
        ),
    )(order, *pieces, *[near(array) for array in (wg, wu, *earlier)])


def begin_loading_kernel(
    order, p0, p1, p2, wg, wu, wd, sum_a, sum_b, near_g, near_u, near_d, rows, row_waits, semaphores
):
    spans = load_spans(wg.shape[0])
    row_copies = [pltpu.make_async_copy(piece, rows.at[n], row_waits.at[n]) for n, piece in enumerate((p0, p1, p2))]
    copies = []
    for p, (start, size) in enumerate(spans):
        span = pl.ds(start, size)
        copies.append(
            [
                pltpu.make_async_copy(wg.at[span, :], near_g.at[span, :], semaphores.at[p, 0]),
                pltpu.make_async_copy(wu.at[span, :], near_u.at[span, :], semaphores.at[p, 1]),
            ]
        )
    copies.append([pltpu.make_async_copy(wd, near_d, semaphores.at[len(spans), 0])])
    for copy in row_copies + copies[0] + copies[1]:
        copy.start()
    for copy in row_copies:
        copy.wait()
    for p, (begin, length) in enumerate(spans):
        for copy in copies[p]:
            copy.wait()
        if p + 2 < len(copies):
            for copy in copies[p + 2]:
                copy.start()
        for start, size in tiles(length):
            part = slice(begin + start, begin + start + size)
            sum_a[:, part], sum_b[:, part] = piece_sums(
                order, 0, [rows.at[n] for n in range(3)], near_g, near_u, part
            )
    copies[-1][0].wait()


def begin_loading(order, pieces, weights):
    rows, quarter = pieces[0].shape
    units = weights[0].shape[0]
    return pl.pallas_call(
        begin_loading_kernel,
        in_specs=[SMEM] + [ANY] * 6,
        out_specs=[VMEM] * 5,
        out_shape=[pltpu.VMEM((rows, units), F32)] * 2 + [pltpu.VMEM(w.shape, w.dtype) for w in weights],
        scratch_shapes=[
            pltpu.VMEM((3, rows, quarter), BF16),
            pltpu.SemaphoreType.DMA((3,)),
            pltpu.SemaphoreType.DMA((len(load_spans(units)) + 1, 2)),
        ],
        compiler_params=params(),
        cost_estimate=pl.CostEstimate(
            flops=12 * rows * quarter * units, bytes_accessed=12 * units * quarter, transcendentals=0
        ),
    )(order, *pieces, *[far(w) for w in weights])


def finish_kernel(order, top, bottom, sum_a, sum_b, wg, wu, hidden, opposite):
    half = top.shape[0]
    opposite[:half] = top[...]
    opposite[half:] = bottom[...]
    for start, size in tiles(wg.shape[0]):
        part = slice(start, start + size)
        a, b = piece_sums(order, 3, (opposite,), wg, wu, part)
        a += sum_a[:, part]
        b += sum_b[:, part]
        hidden[:, part] = (a * jax.nn.sigmoid(a) * b).astype(BF16)


def finish(order, halves, sums, wg, wu):
    rows, units = sums[0].shape
    quarter = halves[0].shape[1]
    return pl.pallas_call(
        finish_kernel,
        in_specs=[SMEM] + [VMEM] * 6,
        out_specs=VMEM,
        out_shape=pltpu.VMEM((rows, units), BF16),
        scratch_shapes=[pltpu.VMEM((rows, quarter), BF16)],
        compiler_params=params(),
        cost_estimate=pl.CostEstimate(
            flops=4 * rows * quarter * units, bytes_accessed=4 * units * quarter, transcendentals=rows * units
        ),
    )(order, *halves, *[near(array) for array in (*sums, wg, wu)])


def load_spans(units):
    cuts = [0, min(256, units), min(512, units), min(896, units), units]
    return [(low, high - low) for low, high in zip(cuts, cuts[1:]) if high > low]


def middle_kernel(order, top, bottom, sum_a, sum_b, c, wg, wu, wd, da, db, result_top, result_bottom, opposite):
    half, quarter = top.shape
    opposite[:half] = top[...]
    opposite[half:] = bottom[...]
    for start, size in tiles(wg.shape[0]):
        part = slice(start, start + size)
        a, b = piece_sums(order, 3, (opposite,), wg, wu, part)
        a += sum_a[:, part]
        b += sum_b[:, part]
        q = jax.nn.sigmoid(a)
        dh = contract_last(c[...], wd[part, :])
        da[:, part] = (dh * (b * q * (1.0 + a * (1.0 - q)))).astype(BF16)
        db[:, part] = (dh * (a * q)).astype(BF16)
    slots = columns(order[3], quarter)
    result = jnp.dot(da[...], wg[:, slots], preferred_element_type=F32)
    result += jnp.dot(db[...], wu[:, slots], preferred_element_type=F32)
    result_top[...] = result[:half].astype(BF16)
    result_bottom[...] = result[half:].astype(BF16)


def middle(order, halves, sums, c, weights):
    rows, units = sums[0].shape
    half, quarter = halves[0].shape
    result = jax.ShapeDtypeStruct((half, quarter), BF16)
    return pl.pallas_call(
        middle_kernel,
        in_specs=[SMEM] + [VMEM] * 8,
        out_specs=[VMEM] * 4,
        out_shape=[pltpu.VMEM((rows, units), BF16)] * 2 + [result] * 2,
        scratch_shapes=[pltpu.VMEM((rows, quarter), BF16)],
        compiler_params=params(),
        cost_estimate=pl.CostEstimate(
            flops=16 * rows * quarter * units, bytes_accessed=16 * units * quarter, transcendentals=rows * units
        ),
    )(order, *halves, *[near(array) for array in sums], c, *[near(array) for array in weights])


def whole_kernel(order, act, weight, out, mark, results, semaphores):
    quarter = results.shape[-1]
    copies = []
    for n in range(4):
        slots = slice(n * quarter, (n + 1) * quarter)
        results[n] = jnp.dot(act[...], weight[:, slots], preferred_element_type=F32).astype(BF16)
        copies.append(
            pltpu.make_async_copy(results.at[n], out.at[:, pl.ds(n * quarter, quarter)], semaphores.at[n])
        )
        copies[n].start()
    mark[...] = jnp.zeros_like(mark)
    for copy in copies:
        copy.wait()


def whole_result(order, act, weight):
    rows, units = act.shape
    features = weight.shape[1]
    return pl.pallas_call(
        whole_kernel,
        in_specs=[SMEM] + [VMEM] * 2,
        out_specs=[ANY, VMEM],
        out_shape=[pltpu.HBM((rows, features), BF16), jax.ShapeDtypeStruct((8, 128), F32)],
        scratch_shapes=[pltpu.VMEM((4, rows, features // 4), BF16), pltpu.SemaphoreType.DMA((4,))],
        compiler_params=params(),
        cost_estimate=pl.CostEstimate(
            flops=2 * rows * units * features, bytes_accessed=2 * units * features, transcendentals=0
        ),
    )(order, near(act), near(weight))


def down_kernel(which, pairs, order, *refs):
    acts, weights, outs = refs[:pairs], refs[pairs : 2 * pairs], refs[2 * pairs :]
    quarter = weights[0].shape[1] // 4
    for n, entry in enumerate(which):
        slots = columns(order[entry], quarter)
        total = functools.reduce(
            jnp.add, [jnp.dot(a[...], w[:, slots], preferred_element_type=F32) for a, w in zip(acts, weights)]
        )
        outs[n][...] = total.astype(outs[n].dtype)


def down_projections(order, which, acts, weights, outs):
    rows, units = acts[0].shape
    quarter = weights[0].shape[1] // 4
    pairs = len(acts)
    return pl.pallas_call(
        functools.partial(down_kernel, which, pairs),
        in_specs=[SMEM] + [VMEM] * (2 * pairs),
        out_specs=[VMEM] * len(outs),
        out_shape=outs,
        compiler_params=params(),
        cost_estimate=pl.CostEstimate(
            flops=2 * len(which) * pairs * rows * units * quarter,
            bytes_accessed=2 * len(which) * pairs * units * quarter,
            transcendentals=0,
        ),
    )(order, *[near(array) for array in (*acts, *weights)])


def passed_kernel(to_next, to_last, up, down, next_sum, last_sum):
    half = up.shape[0]
    next_sum[:half] = (to_next[:half].astype(F32) + up[...].astype(F32)).astype(BF16)
    next_sum[half:] = to_next[half:]
    last_sum[:half] = to_last[:half]
    last_sum[half:] = (to_last[half:].astype(F32) + down[...].astype(F32)).astype(BF16)


def total_kernel(own, from_last, from_next, out):
    out[...] = (own[...] + from_last[...].astype(F32) + from_next[...].astype(F32)).astype(BF16)


def summed_over_tensor(order, top, bottom, acts, weights, earlier):
    rows = acts[0].shape[0]
    quarter = weights[0].shape[1] // 4
    whole = jax.ShapeDtypeStruct((rows, quarter), BF16)
    up = shift(top, "tensor", 1)
    down = shift(bottom, "tensor", -1)
    kept = [pltpu.VMEM(whole.shape, BF16)] * 2 + [pltpu.VMEM(whole.shape, F32)]
    to_next, to_last, own = down_projections(order, (2, 1, 0), acts, weights, kept)
    to_next, to_last = pl.pallas_call(passed_kernel, out_shape=[whole, whole], compiler_params=params())(
        near(to_next), near(to_last), up, down
    )
    from_last = shift(to_next, "tensor", 1)
    from_next = shift(to_last, "tensor", -1)
    from_next = after(from_next, *earlier)
    return pl.pallas_call(total_kernel, out_shape=whole, compiler_params=params())(near(own), from_last, from_next)


def mix(table, back):
    both = lax.dot_general(table, back, (((0,), (0,)), ((), ())), preferred_element_type=F32)
    tokens = both.shape[0] // 2
    return both[:tokens] + both[tokens:]


def mix_kernel(table, back, residual, out):
    out[...] = (residual[...].astype(F32) + mix(table[...], back[...])).astype(BF16)


def mixed(table, back, residual):
    return pl.pallas_call(
        mix_kernel, out_shape=jax.ShapeDtypeStruct(residual.shape, BF16), compiler_params=params()
    )(table, back, residual)


def mix_parts_kernel(order, table, back, residual, own, to_last, to_next, to_opposite):
    quarter = residual.shape[1]
    own[...] = residual[...].astype(F32) + mix(table[...], back[:, columns(order[0], quarter)])
    for entry, out in ((1, to_last), (2, to_next), (3, to_opposite)):
        out[...] = mix(table[...], back[:, columns(order[entry], quarter)]).astype(BF16)


def mixed_over_tensor(order, table, back, residual):
    part = jax.ShapeDtypeStruct(residual.shape, BF16)
    own, to_last, to_next, to_opposite = pl.pallas_call(
        mix_parts_kernel,
        in_specs=[SMEM] + [VMEM] * 3,
        out_specs=[VMEM] * 4,
        out_shape=[jax.ShapeDtypeStruct(residual.shape, F32), part, part, part],
        compiler_params=params(),
    )(order, table, back, residual)
    return own, to_last, to_next, to_opposite


def total_over_tensor(own, to_last, to_next, to_opposite):
    received = (shift(to_last, "tensor", -1), shift(to_next, "tensor", 1), shift(to_opposite, "tensor", 2))
    return (own + sum(piece.astype(F32) for piece in received)).astype(BF16)


def exchange(rows):
    return lax.all_to_all(rows, "expert", split_axis=0, concat_axis=0, tiled=True)


def local(fwd_in, bwd_in, cotangent, route_fwd, gate_fwd, route_bwd, gate_bwd, w_gate, w_up, w_down):
    experts = lax.axis_size("expert")
    f, x, c = fwd_in[0], bwd_in[0], cotangent[0]
    tokens, quarter = f.shape
    fanout = route_fwd.shape[2]
    capacity = min(tokens, max(2, tokens * fanout * 3 // (2 * experts)))
    place = lax.axis_index("tensor").astype(jnp.int32)
    order = (place + jnp.array([0, 3, 1, 2], jnp.int32)) % 4

    c_pieces = (c, shift(c, "tensor", 1), shift(c, "tensor", -1), shift(c, "tensor", 2))
    send, table_b, mix_f, mix_b = dispatch(
        route_fwd[0].T, gate_fwd[0].T, route_bwd[0].T, gate_bwd[0].T, f, x, experts, capacity
    )
    wg, wu, wd = w_gate[0, 0], w_up[0, 0], w_down[0, 0]
    got = exchange(send)
    send_c = dispatch_whole(order, table_b, c_pieces)
    got, send_c = lax.optimization_barrier((got, send_c))
    f0, x0 = got[:, :quarter], got[:, quarter:]
    rows_c = exchange(after(send_c, f0, x0))
    f_last, f_next = shift(f0, "tensor", 1), shift(f0, "tensor", -1)
    near_g, near_u, near_d, loaded = load_weights((wg, wu, wd))
    *sums, _ = begin(order, 0, (f0,), near_g, near_u, ())
    f_top, f_bottom = halves(f_last, f_next, loaded)
    f_opposite = shift(f_top, "tensor", 1), shift(f_bottom, "tensor", -1)
    *sums, begun = begin(order, 1, (f_last, f_next), near_g, near_u, sums)
    x0 = held(x0, f_top, f_bottom, begun)
    x_next, x_last = shift(x0, "tensor", -1), shift(x0, "tensor", 1)
    x_top, x_bottom = halves(x_last, x_next)
    x_opposite = shift(x_top, "tensor", 1), shift(x_bottom, "tensor", -1)

    hidden = finish(order, f_opposite, sums, near_g, near_u)
    part_f, sent = whole_result(order, hidden, near_d)
    back_f = exchange(part_f)
    *sums, near_g, near_u, near_d = begin_loading(order, (held(x0, sent), x_last, x_next), (wg, wu, wd))
    da, db, top, bottom = middle(order, x_opposite, sums, rows_c, (near_g, near_u, near_d))
    mixed_f = mixed_over_tensor(order, mix_f, back_f, f)
    share_b = summed_over_tensor(order, top, bottom, (da, db), (near_g, near_u), mixed_f)
    out_f = total_over_tensor(*mixed_f)
    out_b = mixed(mix_b, exchange(share_b), c)
    return shift(out_f[None], "pipe", 1), shift(out_b[None], "pipe", -1)


def solution(mesh):
    rows = P("pipe", "expert", "tensor")
    routes = P("pipe", "expert", None)
    weights = P("pipe", "expert", "tensor", None)
    return jax.shard_map(
        local,
        mesh=mesh,
        in_specs=(rows, rows, rows, routes, routes, routes, routes, weights, weights, weights),
        out_specs=(rows, rows),
        check_vma=False,
    )
```

```python
import functools

import jax
import jax.numpy as jnp
from jax import lax
from jax.experimental import pallas as pl
from jax.experimental.pallas import tpu as pltpu
from jax.sharding import PartitionSpec as P

F32 = jnp.float32
BF16 = jnp.bfloat16
VMEM = pl.BlockSpec(memory_space=pltpu.VMEM)
SMEM = pl.BlockSpec(memory_space=pltpu.SMEM)
ANY = pl.BlockSpec(memory_space=pl.ANY)


def params(mebibytes=8):
    return pltpu.CompilerParams(vmem_limit_bytes=mebibytes * 1024 * 1024)


def near(array):
    return pltpu.with_memory_space_constraint(array, pltpu.VMEM)


def far(array):
    return pltpu.with_memory_space_constraint(array, pltpu.HBM)


def contract_last(rows, weight):
    return lax.dot_general(rows, weight, (((1,), (1,)), ((), ())), preferred_element_type=F32)


def shift(shard, axis, by):
    length = lax.axis_size(axis)
    return lax.ppermute(shard, axis, [(i, (i + by) % length) for i in range(length)])


def after(value, *earlier):
    return lax.optimization_barrier((value, *earlier))[0]


def slot_tables(route, gate, experts, capacity):
    fanout, tokens = route.shape
    slots = experts * capacity
    labels = lax.broadcasted_iota(jnp.int32, (experts, tokens), 0)
    picks = [(route[k : k + 1, :] == labels).astype(F32) for k in range(fanout)]
    member = functools.reduce(jnp.add, picks)
    row = lax.broadcasted_iota(jnp.int32, (tokens, tokens), 0)
    column = lax.broadcasted_iota(jnp.int32, (tokens, tokens), 1)
    earlier = (row < column).astype(BF16)
    rank = jnp.dot(member.astype(BF16), earlier, preferred_element_type=F32)
    place = rank + (labels * capacity).astype(F32)
    slot_ids = lax.broadcasted_iota(jnp.int32, (slots, tokens), 0)
    table = jnp.zeros((slots, tokens), F32)
    high = jnp.zeros((slots, tokens), F32)
    low = jnp.zeros((slots, tokens), F32)
    for k in range(fanout):
        target = jnp.sum(picks[k] * place, axis=0, keepdims=True).astype(jnp.int32)
        hit = (slot_ids == target).astype(F32)
        gate_k = gate[k : k + 1, :]
        high_k = ((gate_k >> 7) << 7).astype(F32) * (1.0 / 65536.0)
        low_k = (gate_k & 127).astype(F32) * (1.0 / 65536.0)
        table += hit
        high += hit * high_k
        low += hit * low_k
    return table.astype(BF16), jnp.concatenate([high, low], axis=1).astype(BF16)


def dispatch_kernel(experts, capacity, rf, gf, rb, gb, f, x, send, table_b, mix_f, mix_b):
    quarter = f.shape[1]
    table, mix_f[...] = slot_tables(rf[...], gf[...], experts, capacity)
    send[:, :quarter] = jnp.dot(table, f[...], preferred_element_type=F32).astype(BF16)
    table, mix_b[...] = slot_tables(rb[...], gb[...], experts, capacity)
    table_b[...] = table
    send[:, quarter:] = jnp.dot(table, x[...], preferred_element_type=F32).astype(BF16)


def dispatch(rf, gf, rb, gb, f, x, experts, capacity):
    tokens, quarter = f.shape
    slots = experts * capacity
    return pl.pallas_call(
        functools.partial(dispatch_kernel, experts, capacity),
        out_shape=(
            pltpu.HBM((slots, 2 * quarter), BF16),
            pltpu.HBM((slots, tokens), BF16),
            pltpu.HBM((slots, 2 * tokens), BF16),
            pltpu.HBM((slots, 2 * tokens), BF16),
        ),
        compiler_params=params(),
    )(*[far(array) for array in (rf, gf, rb, gb, f, x)])


def dispatch_whole_kernel(order, table, p0, p1, p2, p3, send):
    quarter = p0.shape[1]
    for n, piece in enumerate((p0, p1, p2, p3)):
        rows = jnp.dot(table[...], piece[...], preferred_element_type=F32).astype(BF16)
        send[:, pl.ds(pl.multiple_of(order[n] * quarter, quarter), quarter)] = rows


def dispatch_whole(order, table, pieces):
    slots = table.shape[0]
    features = 4 * pieces[0].shape[1]
    return pl.pallas_call(
        dispatch_whole_kernel,
        in_specs=[SMEM] + [VMEM] * 5,
        out_specs=VMEM,
        out_shape=pltpu.HBM((slots, features), BF16),
        compiler_params=params(),
    )(order, table, *pieces)


def tiles(units, tile=256):
    return [(start, min(tile, units - start)) for start in range(0, units, tile)]


def columns(number, quarter):
    return pl.ds(pl.multiple_of(number * quarter, quarter), quarter)


def load_kernel(*refs):
    count = (len(refs) - 2) // 2
    mark, semaphores = refs[-2:]
    copies = [pltpu.make_async_copy(refs[n], refs[count + n], semaphores.at[n]) for n in range(count)]
    for copy in copies:
        copy.start()
    mark[...] = jnp.zeros_like(mark)
    for copy in copies:
        copy.wait()


def load_weights(weights):
    return pl.pallas_call(
        load_kernel,
        in_specs=[ANY] * len(weights),
        out_specs=[VMEM] * (len(weights) + 1),
        out_shape=[pltpu.VMEM(weight.shape, weight.dtype) for weight in weights]
        + [jax.ShapeDtypeStruct((8, 128), F32)],
        scratch_shapes=[pltpu.SemaphoreType.DMA((len(weights),))],
        compiler_params=params(2),
        cost_estimate=pl.CostEstimate(
            flops=0, bytes_accessed=sum(weight.size * 2 for weight in weights), transcendentals=0
        ),
    )(*[far(weight) for weight in weights])


def held_kernel(*refs):
    pass


def held(array, *earlier):
    return pl.pallas_call(
        held_kernel,
        in_specs=[ANY] * (1 + len(earlier)),
        out_specs=ANY,
        out_shape=jax.ShapeDtypeStruct(array.shape, array.dtype),
        input_output_aliases={0: 0},
        compiler_params=params(2),
        cost_estimate=pl.CostEstimate(flops=0, bytes_accessed=16 * 1024 * 1024, transcendentals=0),
    )(array, *earlier)


def halves_kernel(from_last, from_next, *refs):
    top, bottom = refs[-2:]
    half = top.shape[0]
    top[...] = from_last[:half]
    bottom[...] = from_next[half:]


def halves(from_last, from_next, *earlier):
    rows, quarter = from_last.shape
    return pl.pallas_call(
        halves_kernel,
        in_specs=[VMEM] * 2 + [ANY] * len(earlier),
        out_specs=[VMEM] * 2,
        out_shape=[jax.ShapeDtypeStruct((rows // 2, quarter), from_last.dtype)] * 2,
        compiler_params=params(4),
    )(from_last, from_next, *earlier)


def piece_sums(order, first_entry, pieces, wg, wu, part):
    quarter = pieces[0].shape[1]
    sums = []
    for weight in (wg, wu):
        terms = [
            contract_last(piece[...], weight[part, columns(order[first_entry + n], quarter)])
            for n, piece in enumerate(pieces)
        ]
        sums.append(functools.reduce(jnp.add, terms))
    return sums


def begin_kernel(first_entry, count, order, *refs):
    pieces, (wg, wu), earlier, (sum_a, sum_b, mark) = refs[:count], refs[count : count + 2], refs[count + 2 : -3], refs[-3:]
    mark[...] = jnp.zeros_like(mark)
    for start, size in tiles(wg.shape[0]):
        part = slice(start, start + size)
        a, b = piece_sums(order, first_entry, pieces, wg, wu, part)
        if earlier:
            a += earlier[0][:, part]
            b += earlier[1][:, part]
        sum_a[:, part] = a
        sum_b[:, part] = b


def begin(order, first_entry, pieces, wg, wu, earlier):
    rows, quarter = pieces[0].shape
    units = wg.shape[0]
    count = len(pieces)
    return pl.pallas_call(
        functools.partial(begin_kernel, first_entry, count),
        in_specs=[SMEM] + [VMEM] * (count + 2 + len(earlier)),
        out_specs=[VMEM] * 3,
        out_shape=[pltpu.VMEM((rows, units), F32)] * 2 + [jax.ShapeDtypeStruct((8, 128), F32)],
        compiler_params=params(),
        cost_estimate=pl.CostEstimate(
            flops=4 * count * rows * quarter * units, bytes_accessed=4 * count * units * quarter, transcendentals=0
        ),
    )(order, *pieces, *[near(array) for array in (wg, wu, *earlier)])


def begin_loading_kernel(
    order, p0, p1, p2, wg, wu, wd, sum_a, sum_b, near_g, near_u, near_d, rows, row_waits, semaphores
):
    spans = load_spans(wg.shape[0])
    row_copies = [pltpu.make_async_copy(piece, rows.at[n], row_waits.at[n]) for n, piece in enumerate((p0, p1, p2))]
    copies = []
    for p, (start, size) in enumerate(spans):
        span = pl.ds(start, size)
        copies.append(
            [
                pltpu.make_async_copy(wg.at[span, :], near_g.at[span, :], semaphores.at[p, 0]),
                pltpu.make_async_copy(wu.at[span, :], near_u.at[span, :], semaphores.at[p, 1]),
            ]
        )
    copies.append([pltpu.make_async_copy(wd, near_d, semaphores.at[len(spans), 0])])
    for copy in row_copies + copies[0] + copies[1]:
        copy.start()
    for copy in row_copies:
        copy.wait()
    for p, (begin, length) in enumerate(spans):
        for copy in copies[p]:
            copy.wait()
        if p + 2 < len(copies):
            for copy in copies[p + 2]:
                copy.start()
        for start, size in tiles(length):
            part = slice(begin + start, begin + start + size)
            sum_a[:, part], sum_b[:, part] = piece_sums(
                order, 0, [rows.at[n] for n in range(3)], near_g, near_u, part
            )
    copies[-1][0].wait()


def begin_loading(order, pieces, weights):
    rows, quarter = pieces[0].shape
    units = weights[0].shape[0]
    return pl.pallas_call(
        begin_loading_kernel,
        in_specs=[SMEM] + [ANY] * 6,
        out_specs=[VMEM] * 5,
        out_shape=[pltpu.VMEM((rows, units), F32)] * 2 + [pltpu.VMEM(w.shape, w.dtype) for w in weights],
        scratch_shapes=[
            pltpu.VMEM((3, rows, quarter), BF16),
            pltpu.SemaphoreType.DMA((3,)),
            pltpu.SemaphoreType.DMA((len(load_spans(units)) + 1, 2)),
        ],
        compiler_params=params(),
        cost_estimate=pl.CostEstimate(
            flops=12 * rows * quarter * units, bytes_accessed=12 * units * quarter, transcendentals=0
        ),
    )(order, *pieces, *[far(w) for w in weights])


def finish_kernel(order, top, bottom, sum_a, sum_b, wg, wu, hidden, opposite):
    half = top.shape[0]
    opposite[:half] = top[...]
    opposite[half:] = bottom[...]
    for start, size in tiles(wg.shape[0]):
        part = slice(start, start + size)
        a, b = piece_sums(order, 3, (opposite,), wg, wu, part)
        a += sum_a[:, part]
        b += sum_b[:, part]
        hidden[:, part] = (a * jax.nn.sigmoid(a) * b).astype(BF16)


def finish(order, halves, sums, wg, wu):
    rows, units = sums[0].shape
    quarter = halves[0].shape[1]
    return pl.pallas_call(
        finish_kernel,
        in_specs=[SMEM] + [VMEM] * 6,
        out_specs=VMEM,
        out_shape=pltpu.VMEM((rows, units), BF16),
        scratch_shapes=[pltpu.VMEM((rows, quarter), BF16)],
        compiler_params=params(),
        cost_estimate=pl.CostEstimate(
            flops=4 * rows * quarter * units, bytes_accessed=4 * units * quarter, transcendentals=rows * units
        ),
    )(order, *halves, *[near(array) for array in (*sums, wg, wu)])


def load_spans(units):
    cuts = [0, min(256, units), min(512, units), min(896, units), units]
    return [(low, high - low) for low, high in zip(cuts, cuts[1:]) if high > low]


def middle_kernel(order, top, bottom, sum_a, sum_b, c, wg, wu, wd, da, db, result_top, result_bottom, opposite):
    half, quarter = top.shape
    opposite[:half] = top[...]
    opposite[half:] = bottom[...]
    for start, size in tiles(wg.shape[0]):
        part = slice(start, start + size)
        a, b = piece_sums(order, 3, (opposite,), wg, wu, part)
        a += sum_a[:, part]
        b += sum_b[:, part]
        q = jax.nn.sigmoid(a)
        dh = contract_last(c[...], wd[part, :])
        da[:, part] = (dh * (b * q * (1.0 + a * (1.0 - q)))).astype(BF16)
        db[:, part] = (dh * (a * q)).astype(BF16)
    slots = columns(order[3], quarter)
    result = jnp.dot(da[...], wg[:, slots], preferred_element_type=F32)
    result += jnp.dot(db[...], wu[:, slots], preferred_element_type=F32)
    result_top[...] = result[:half].astype(BF16)
    result_bottom[...] = result[half:].astype(BF16)


def middle(order, halves, sums, c, weights):
    rows, units = sums[0].shape
    half, quarter = halves[0].shape
    result = jax.ShapeDtypeStruct((half, quarter), BF16)
    return pl.pallas_call(
        middle_kernel,
        in_specs=[SMEM] + [VMEM] * 8,
        out_specs=[VMEM] * 4,
        out_shape=[pltpu.VMEM((rows, units), BF16)] * 2 + [result] * 2,
        scratch_shapes=[pltpu.VMEM((rows, quarter), BF16)],
        compiler_params=params(),
        cost_estimate=pl.CostEstimate(
            flops=16 * rows * quarter * units, bytes_accessed=16 * units * quarter, transcendentals=rows * units
        ),
    )(order, *halves, *[near(array) for array in sums], c, *[near(array) for array in weights])


def whole_kernel(order, act, weight, out, mark, results, semaphores):
    quarter = results.shape[-1]
    copies = []
    for n in range(4):
        slots = slice(n * quarter, (n + 1) * quarter)
        results[n] = jnp.dot(act[...], weight[:, slots], preferred_element_type=F32).astype(BF16)
        copies.append(
            pltpu.make_async_copy(results.at[n], out.at[:, pl.ds(n * quarter, quarter)], semaphores.at[n])
        )
        copies[n].start()
    mark[...] = jnp.zeros_like(mark)
    for copy in copies:
        copy.wait()


def whole_result(order, act, weight):
    rows, units = act.shape
    features = weight.shape[1]
    return pl.pallas_call(
        whole_kernel,
        in_specs=[SMEM] + [VMEM] * 2,
        out_specs=[ANY, VMEM],
        out_shape=[pltpu.HBM((rows, features), BF16), jax.ShapeDtypeStruct((8, 128), F32)],
        scratch_shapes=[pltpu.VMEM((4, rows, features // 4), BF16), pltpu.SemaphoreType.DMA((4,))],
        compiler_params=params(),
        cost_estimate=pl.CostEstimate(
            flops=2 * rows * units * features, bytes_accessed=2 * units * features, transcendentals=0
        ),
    )(order, near(act), near(weight))


def sides_kernel(order, da, db, wg, wu, next_top, next_bottom, last_top, last_bottom):
    half, quarter = next_top.shape
    for entry, top, bottom in ((2, next_top, next_bottom), (1, last_top, last_bottom)):
        result = feature_slice(order[entry], (da, db), (wg, wu), quarter).astype(BF16)
        top[...] = result[:half]
        bottom[...] = result[half:]


def own_kernel(order, da, db, wg, wu, own):
    own[...] = feature_slice(order[0], (da, db), (wg, wu), own.shape[1])


def feature_slice(place, acts, weights, quarter):
    slots = columns(place, quarter)
    return functools.reduce(
        jnp.add, [jnp.dot(a[...], w[:, slots], preferred_element_type=F32) for a, w in zip(acts, weights)]
    )


def result_slices(kernel, order, acts, weights, slices, outs):
    rows, units = acts[0].shape
    quarter = weights[0].shape[1] // 4
    return pl.pallas_call(
        kernel,
        in_specs=[SMEM] + [VMEM] * 4,
        out_specs=[VMEM] * len(outs),
        out_shape=outs,
        compiler_params=params(),
        cost_estimate=pl.CostEstimate(
            flops=4 * slices * rows * units * quarter, bytes_accessed=4 * slices * units * quarter, transcendentals=0
        ),
    )(order, *[near(array) for array in (*acts, *weights)])


def passed_kernel(next_top, last_bottom, up, down, next_sum, last_sum):
    next_sum[...] = (next_top[...].astype(F32) + up[...].astype(F32)).astype(BF16)
    last_sum[...] = (last_bottom[...].astype(F32) + down[...].astype(F32)).astype(BF16)


def total_kernel(own, last_top, last_bottom, next_top, next_bottom, out):
    half = last_top.shape[0]
    tops = last_top[...].astype(F32) + next_top[...].astype(F32)
    bottoms = last_bottom[...].astype(F32) + next_bottom[...].astype(F32)
    out[:half] = (own[:half] + tops).astype(BF16)
    out[half:] = (own[half:] + bottoms).astype(BF16)


def summed_over_tensor(order, top, bottom, acts, weights, earlier):
    rows = acts[0].shape[0]
    quarter = weights[0].shape[1] // 4
    half = jax.ShapeDtypeStruct((rows // 2, quarter), BF16)
    kept = pltpu.VMEM(half.shape, BF16)
    up = shift(top, "tensor", 1)
    down = shift(bottom, "tensor", -1)
    next_top, next_bottom, last_top, last_bottom = result_slices(
        sides_kernel, order, acts, weights, 2, [kept, half, half, kept]
    )
    from_last_bottom = shift(next_bottom, "tensor", 1)
    from_next_top = shift(last_top, "tensor", -1)
    (own,) = result_slices(own_kernel, order, acts, weights, 1, [pltpu.VMEM((rows, quarter), F32)])
    next_top, last_bottom = pl.pallas_call(passed_kernel, out_shape=[half, half], compiler_params=params())(
        near(next_top), near(last_bottom), up, down
    )
    from_last_top = shift(next_top, "tensor", 1)
    from_next_bottom = shift(last_bottom, "tensor", -1)
    from_next_bottom = after(from_next_bottom, *earlier)
    return pl.pallas_call(
        total_kernel, out_shape=jax.ShapeDtypeStruct((rows, quarter), BF16), compiler_params=params()
    )(near(own), from_last_top, from_last_bottom, from_next_top, from_next_bottom)


def mix(table, back):
    both = lax.dot_general(table, back, (((0,), (0,)), ((), ())), preferred_element_type=F32)
    tokens = both.shape[0] // 2
    return both[:tokens] + both[tokens:]


def mix_kernel(table, back, residual, out):
    out[...] = (residual[...].astype(F32) + mix(table[...], back[...])).astype(BF16)


def mixed(table, back, residual):
    return pl.pallas_call(
        mix_kernel, out_shape=jax.ShapeDtypeStruct(residual.shape, BF16), compiler_params=params()
    )(table, back, residual)


def mix_parts_kernel(order, table, back, residual, own, to_last, to_next, to_opposite):
    quarter = residual.shape[1]
    own[...] = residual[...].astype(F32) + mix(table[...], back[:, columns(order[0], quarter)])
    for entry, out in ((1, to_last), (2, to_next), (3, to_opposite)):
        out[...] = mix(table[...], back[:, columns(order[entry], quarter)]).astype(BF16)


def mixed_over_tensor(order, table, back, residual):
    part = jax.ShapeDtypeStruct(residual.shape, BF16)
    own, to_last, to_next, to_opposite = pl.pallas_call(
        mix_parts_kernel,
        in_specs=[SMEM] + [VMEM] * 3,
        out_specs=[VMEM] * 4,
        out_shape=[jax.ShapeDtypeStruct(residual.shape, F32), part, part, part],
        compiler_params=params(),
    )(order, table, back, residual)
    return own, to_last, to_next, to_opposite


def total_over_tensor(own, to_last, to_next, to_opposite):
    received = (shift(to_last, "tensor", -1), shift(to_next, "tensor", 1), shift(to_opposite, "tensor", 2))
    return (own + sum(piece.astype(F32) for piece in received)).astype(BF16)


def exchange(rows):
    return lax.all_to_all(rows, "expert", split_axis=0, concat_axis=0, tiled=True)


def local(fwd_in, bwd_in, cotangent, route_fwd, gate_fwd, route_bwd, gate_bwd, w_gate, w_up, w_down):
    experts = lax.axis_size("expert")
    f, x, c = fwd_in[0], bwd_in[0], cotangent[0]
    tokens, quarter = f.shape
    fanout = route_fwd.shape[2]
    capacity = min(tokens, max(2, tokens * fanout * 3 // (2 * experts)))
    place = lax.axis_index("tensor").astype(jnp.int32)
    order = (place + jnp.array([0, 3, 1, 2], jnp.int32)) % 4

    c_pieces = (c, shift(c, "tensor", 1), shift(c, "tensor", -1), shift(c, "tensor", 2))
    send, table_b, mix_f, mix_b = dispatch(
        route_fwd[0].T, gate_fwd[0].T, route_bwd[0].T, gate_bwd[0].T, f, x, experts, capacity
    )
    wg, wu, wd = w_gate[0, 0], w_up[0, 0], w_down[0, 0]
    got = exchange(send)
    send_c = dispatch_whole(order, table_b, c_pieces)
    got, send_c = lax.optimization_barrier((got, send_c))
    f0, x0 = got[:, :quarter], got[:, quarter:]
    rows_c = exchange(after(send_c, f0, x0))
    f_last, f_next = shift(f0, "tensor", 1), shift(f0, "tensor", -1)
    near_g, near_u, near_d, loaded = load_weights((wg, wu, wd))
    *sums, _ = begin(order, 0, (f0,), near_g, near_u, ())
    f_top, f_bottom = halves(f_last, f_next, loaded)
    f_opposite = shift(f_top, "tensor", 1), shift(f_bottom, "tensor", -1)
    *sums, begun = begin(order, 1, (f_last, f_next), near_g, near_u, sums)
    x0 = held(x0, f_top, f_bottom, begun)
    x_next, x_last = shift(x0, "tensor", -1), shift(x0, "tensor", 1)
    x_top, x_bottom = halves(x_last, x_next)
    x_opposite = shift(x_top, "tensor", 1), shift(x_bottom, "tensor", -1)

    hidden = finish(order, f_opposite, sums, near_g, near_u)
    part_f, sent = whole_result(order, hidden, near_d)
    back_f = exchange(part_f)
    *sums, near_g, near_u, near_d = begin_loading(order, (held(x0, sent), x_last, x_next), (wg, wu, wd))
    da, db, top, bottom = middle(order, x_opposite, sums, rows_c, (near_g, near_u, near_d))
    mixed_f = mixed_over_tensor(order, mix_f, back_f, f)
    share_b = summed_over_tensor(order, top, bottom, (da, db), (near_g, near_u), mixed_f)
    out_f = total_over_tensor(*mixed_f)
    out_b = mixed(mix_b, exchange(share_b), c)
    return shift(out_f[None], "pipe", 1), shift(out_b[None], "pipe", -1)


def solution(mesh):
    rows = P("pipe", "expert", "tensor")
    routes = P("pipe", "expert", None)
    weights = P("pipe", "expert", "tensor", None)
    return jax.shard_map(
        local,
        mesh=mesh,
        in_specs=(rows, rows, rows, routes, routes, routes, routes, weights, weights, weights),
        out_specs=(rows, rows),
        check_vma=False,
    )
```
